32 devices in a mesh: rep: 2 (over x), grp: 8 (over z, y), mem: 2 (over core).
Axes of the slice: x: 2, y: 2, z: 4, core: 2. Of those that a mesh axis runs over, the one named last changes fastest.
Arguments:
- layer_input: bfloat16 [4096, 2048], P(('rep', 'grp', 'mem')), parts along dimension 0, may hold values from -6 to 6
- output_grad: bfloat16 [4096, 2048], P(('rep', 'grp', 'mem')), parts along dimension 0, may hold values from -24 to 24
- expert_ids: int32 [4096, 8], P(('rep', 'grp', 'mem')), parts along dimension 0, may hold values from 0 to 15, all different within a row; in each aligned block of 128 rows (0 to 127, 128 to 255, ...) at most 72 rows name the same one
- route_ints: int32 [4096, 8], P(('rep', 'grp', 'mem')), parts along dimension 0, may hold values from 1 to 255
- w_gate: bfloat16 [16, 2048, 384], P(('grp', 'mem')), may hold values from -0.125 to 0.125
- w_up: bfloat16 [16, 2048, 384], P(('grp', 'mem')), may hold values from -0.125 to 0.125
- w_down: bfloat16 [16, 384, 2048], P(('grp', 'mem')), may hold values from -0.3125 to 0.3125
Outputs:
- input_grad: bfloat16 [4096, 2048], P(('rep', 'grp', 'mem')), parts along dimension 0
- grad_gate: bfloat16 [32, 2048, 384], P(('rep', 'grp', 'mem')), parts along dimension 0
- grad_up: bfloat16 [32, 2048, 384], P(('rep', 'grp', 'mem')), parts along dimension 0
- grad_down: bfloat16 [32, 384, 2048], P(('rep', 'grp', 'mem')), parts along dimension 0
The draws below stay inside these ranges and needn't reach their ends.
There are 2 independent parts, one for each index of `rep`. The reference program is written for one: setup_inputs(seed, part) draws one part's arguments, and reference() takes and returns one part's arrays. A program takes and returns all parts, laid end to end along the dimension named above; an argument that names none is the same for every part. Nothing has to cross between parts.
Inputs may be any that keep to these rules, and one draw needn't show every extreme that they name: `expert_ids`: each row names 8 different experts. The 128 rows of one device name any one expert at most 72 times, and in every draw some device names some expert exactly 72 times.
All inputs are finite; a program needn't handle non-finite values.
Results may differ from the reference program's by a relative error of at most 0.0064.
Values may be sent and summed in bfloat16 or wider, within the bound.
A program may use at most 128 MiB of HBM per device.

```python
import math
import jax
import jax.numpy as jnp
import numpy as np
from jax import lax

D = 2048
FF = 384
TOP = 8
TOK_DEV = 128
EXPERTS = 16
TOKENS = 2048
CAP = 72
N_GRP = 8
N_MEM = 2


def plant(array, own_key, low, largest):
    index_at = [jax.random.randint(jax.random.fold_in(own_key, axis), (), 0, length) for axis, length in enumerate(array.shape)]
    longest = array.shape.index(max(array.shape))
    neighbour = index_at[:longest] + [(index_at[longest] + 1) % array.shape[longest]] + index_at[longest + 1:]
    return array.at[tuple(index_at)].set(low).at[tuple(neighbour)].set(largest)


def levels(rng, extent, split, low, high):
    factor_of = 1.0
    for dim, blocks in split:
        steps = jax.random.uniform(jax.random.fold_in(jax.random.fold_in(rng, 6), dim), (blocks,), jnp.float32, low / len(split), high / len(split))
        factor_of = factor_of * jnp.repeat(jnp.exp(steps), extent[dim] // blocks).reshape((-1,) + (1,) * (len(extent) - 1 - dim))
    return factor_of


def assign_block(stream_key, own, number, rows, count, top, limit, slope):
    order = jax.random.permutation(stream_key, count)
    packed, common = portions_of(count, rows * top, limit, slope, True), portions_of(count, rows * top, limit, slope, False)
    places = jnp.arange(count)

    def named(sizes, rotation):
        used = int((sizes > 0).sum())
        fixed = max(1, used // 4)
        moved = fixed + (places - fixed + rotation * (used - fixed)) % max(1, count - fixed)
        return jnp.zeros((count,), jnp.int32).at[order[jnp.where(places < fixed, places, moved)]].set(jnp.asarray(sizes, jnp.int32))

    sizes = jnp.where(number % 4 == 0, named(packed, number // 4), named(common, number - number // 4 - 1))
    mixed = jax.random.permutation(jax.random.fold_in(own, 3), count)
    donor, receiver = mixed[0:count // 2 * 2:2], mixed[1:count // 2 * 2:2]
    margin = jnp.minimum(sizes[donor] - 1, limit - sizes[receiver]) // 2
    margin = jnp.where((donor == order[0]) | (receiver == order[0]) | (sizes[receiver] == 0), 0, jnp.maximum(margin, 0))
    moved = jax.random.randint(jax.random.fold_in(own, 4), (count // 2,), 0, 1 << 20) % (margin + 1)
    sizes = sizes.at[donor].add(-moved).at[receiver].add(moved)
    labels = jnp.searchsorted(jnp.cumsum(sizes), jnp.arange(rows * top), side="right").astype(jnp.int32)
    listing = labels.reshape(top, rows).T
    listing = listing[jax.random.permutation(jax.random.fold_in(own, 1), rows)]
    rotation = jax.random.randint(jax.random.fold_in(own, 2), (rows, 1), 0, top)
    return jnp.take_along_axis(listing, (jnp.arange(top)[None, :] + rotation) % top, axis=1)


def portions_of(number_of, total, bound, lean, full):
    weights = [(1 << 20) // math.isqrt(rank ** lean) + 1 for rank in range(1, number_of + 1)]
    largest = bound if full else min(bound, max(-(-total // number_of), total * weights[0] // sum(weights)))
    least = 1 if total - largest >= number_of - 1 else 0
    holding, rest = [largest] + [least] * (number_of - 1), total - largest - least * (number_of - 1)
    while rest > 0:
        candidates = [i for i in range(1, number_of) if holding[i] < largest] or [i for i in range(1, number_of) if holding[i] < bound]
        pool, remaining = sum([weights[i] for i in candidates]), rest
        for i in candidates:
            more = min(bound - holding[i], max(1, remaining * weights[i] // pool), rest)
            holding[i] = holding[i] + more
            rest = rest - more
    return np.array(holding)


def scatter_about(stream_key, extent, width, reach, split=(), held_as=jnp.bfloat16):
    drawn = jax.random.normal(stream_key, extent, jnp.float32) * width
    if len(split) > 0:
        drawn = levels(stream_key, extent, split, -0.22, 0.18) * drawn
    return jnp.clip(drawn, min=-reach, max=reach).astype(held_as)


def setup_inputs(seed: int = 0, part: int = 0) -> dict:
    keys = jax.random.split(jax.random.key(seed), 8)
    part_keys = jax.random.split(jax.random.fold_in(keys[7], part), 8)
    layer_input = scatter_about(part_keys[0], (TOKENS, D), 1.0, 6.0, ((0, 16),))
    output_grad = scatter_about(part_keys[1], (TOKENS, D), 4.0, 24.0, ((0, 16),))
    expert_ids_keys = jax.random.split(jax.random.fold_in(part_keys[2], 1), TOKENS // TOK_DEV)
    expert_ids_turns = jax.random.permutation(jax.random.fold_in(part_keys[2], 3), TOKENS // TOK_DEV)
    expert_ids = jax.vmap(lambda own, number: assign_block(jax.random.fold_in(part_keys[2], 2), own, number, TOK_DEV, EXPERTS, TOP, CAP, 2))(expert_ids_keys, expert_ids_turns).reshape((TOKENS, TOP))
    route_ints = plant(jax.random.randint(part_keys[3], (TOKENS, TOP), 1, 256), jax.random.fold_in(part_keys[3], 1), 1, 255).astype(jnp.int32)
    w_gate = scatter_about(keys[4], (EXPERTS, D, FF), D ** -0.5, 0.125, ((0, 16),))
    w_up = scatter_about(keys[5], (EXPERTS, D, FF), D ** -0.5, 0.125, ((0, 16),))
    w_down = scatter_about(keys[6], (EXPERTS, FF, D), FF ** -0.5, 0.3125, ((0, 16),))
    return dict(layer_input=layer_input, output_grad=output_grad, expert_ids=expert_ids, route_ints=route_ints, w_gate=w_gate, w_up=w_up, w_down=w_down)


def reference(layer_input, output_grad, expert_ids, route_ints, w_gate, w_up, w_down):
    tokens = layer_input.shape[0]
    top_count = expert_ids.shape[1]
    pair_count = tokens * top_count
    quotas = route_ints.astype(jnp.float32)
    route_ratio = quotas / jnp.sum(quotas, axis=1, keepdims=True)
    scaled = (route_ratio[:, :, None] * output_grad.astype(jnp.float32)[:, None, :]).astype(jnp.bfloat16)
    scaled = scaled.reshape(pair_count, layer_input.shape[1])
    flat_ids = expert_ids.reshape(pair_count)
    most_rows = N_GRP * N_MEM * CAP

    def per_expert(grad_total, expert):
        picked = jnp.nonzero(flat_ids == expert, size=most_rows, fill_value=pair_count)[0].astype(jnp.int32)
        is_live = picked < pair_count
        safe_pick = jnp.where(is_live, picked, 0).astype(jnp.int32)
        token_index = (safe_pick // top_count).astype(jnp.int32)
        rows_x = jnp.where(is_live[:, None], layer_input[token_index], jnp.zeros((), jnp.bfloat16))
        rows_grad = jnp.where(is_live[:, None], scaled[safe_pick], jnp.zeros((), jnp.bfloat16))
        gate_w = w_gate[expert]
        up_w = w_up[expert]
        down_w = w_down[expert]
        gate_pre = jnp.dot(rows_x, gate_w, preferred_element_type=jnp.float32)
        up_pre = jnp.dot(rows_x, up_w, preferred_element_type=jnp.float32)
        sigmoid_gate = jax.nn.sigmoid(gate_pre)
        activity = gate_pre * sigmoid_gate
        hidden = (activity * up_pre).astype(jnp.bfloat16)
        hidden_grad = jnp.dot(rows_grad, down_w.T, preferred_element_type=jnp.float32)
        up_grad = (hidden_grad * activity).astype(jnp.bfloat16)
        gate_grad = (hidden_grad * up_pre * sigmoid_gate * (1.0 + gate_pre * (1.0 - sigmoid_gate))).astype(jnp.bfloat16)
        down_wgrad = jnp.dot(hidden.T, rows_grad, preferred_element_type=jnp.float32).astype(jnp.bfloat16)
        gate_wgrad = jnp.dot(rows_x.T, gate_grad, preferred_element_type=jnp.float32).astype(jnp.bfloat16)
        up_wgrad = jnp.dot(rows_x.T, up_grad, preferred_element_type=jnp.float32).astype(jnp.bfloat16)
        row_grad = (jnp.dot(gate_grad, gate_w.T, preferred_element_type=jnp.float32)
                    + jnp.dot(up_grad, up_w.T, preferred_element_type=jnp.float32)).astype(jnp.bfloat16)
        target = jnp.where(is_live, token_index, tokens).astype(jnp.int32)
        grad_total = grad_total.at[target].add(row_grad.astype(jnp.float32), mode="drop")
        return grad_total, (gate_wgrad, up_wgrad, down_wgrad)

    start_total = jnp.zeros(layer_input.shape, jnp.float32)
    grad_total, stacked = lax.scan(per_expert, start_total, jnp.arange(EXPERTS, dtype=jnp.int32))
    return grad_total.astype(jnp.bfloat16), stacked[0], stacked[1], stacked[2]
```

```python
import jax
import jax.numpy as jnp
from jax import lax
from jax.experimental import pallas as pl
from jax.experimental.pallas import tpu as pltpu
from jax.sharding import PartitionSpec as P


def routed(layer_input, output_grad, expert_ids, route_ints, w_gate, w_up, w_down):
    devices = lax.axis_size("grp") * lax.axis_size("mem")
    tok_rows = layer_input.shape[0]
    model_width = layer_input.shape[1]
    top_count = expert_ids.shape[1]
    pair_count = tok_rows * top_count
    capacity = max(2, 9 * tok_rows * top_count // (8 * devices))
    slot_count = devices * capacity
    quotas = route_ints.astype(jnp.float32)
    route_ratio = quotas / jnp.sum(quotas, axis=1, keepdims=True)
    scaled = (route_ratio[:, :, None] * output_grad.astype(jnp.float32)[:, None, :]).astype(
        jnp.bfloat16
    )
    scaled = scaled.reshape(pair_count, model_width)
    flat_ids = expert_ids.reshape(pair_count)
    pair_order = jnp.arange(pair_count, dtype=jnp.int32)
    earlier = (flat_ids[None, :] == flat_ids[:, None]) & (pair_order[None, :] < pair_order[:, None])
    slot_rank = jnp.sum(earlier.astype(jnp.int32), axis=1)
    slot_key = flat_ids * capacity + slot_rank
    slot_match = slot_key[None, :] == jnp.arange(slot_count, dtype=jnp.int32)[:, None]
    filled = jnp.any(slot_match, axis=1)
    source_pair = jnp.sum(jnp.where(slot_match, pair_order[None, :], 0), axis=1)
    send_x = jnp.where(
        filled[:, None], layer_input[source_pair // top_count], jnp.zeros((), jnp.bfloat16)
    )
    send_grad = jnp.where(filled[:, None], scaled[source_pair], jnp.zeros((), jnp.bfloat16))
    recv_x, recv_grad = (
        lax.all_to_all(
            send_x.reshape(devices, capacity, model_width),
            ("grp", "mem"),
            split_axis=0,
            concat_axis=0,
            tiled=True,
        ),
        lax.all_to_all(
            send_grad.reshape(devices, capacity, model_width),
            ("grp", "mem"),
            split_axis=0,
            concat_axis=0,
            tiled=True,
        ),
    )
    rows_x = recv_x.reshape(slot_count, model_width)
    rows_grad = recv_grad.reshape(slot_count, model_width)
    gate_w = w_gate[0]
    up_w = w_up[0]
    down_w = w_down[0]
    gate_pre = jnp.dot(rows_x, gate_w, preferred_element_type=jnp.float32)
    up_pre = jnp.dot(rows_x, up_w, preferred_element_type=jnp.float32)
    sigmoid_gate = jax.nn.sigmoid(gate_pre)
    activity = gate_pre * sigmoid_gate
    hidden = (activity * up_pre).astype(jnp.bfloat16)
    hidden_grad = jnp.dot(rows_grad, down_w.T, preferred_element_type=jnp.float32)
    up_grad = (hidden_grad * activity).astype(jnp.bfloat16)
    gate_grad = (
        hidden_grad * up_pre * sigmoid_gate * (1.0 + gate_pre * (1.0 - sigmoid_gate))
    ).astype(jnp.bfloat16)
    row_grad = (
        jnp.dot(gate_grad, gate_w.T, preferred_element_type=jnp.float32)
        + jnp.dot(up_grad, up_w.T, preferred_element_type=jnp.float32)
    ).astype(jnp.bfloat16)
    returned = lax.all_to_all(
        row_grad.reshape(devices, capacity, model_width),
        ("grp", "mem"),
        split_axis=0,
        concat_axis=0,
        tiled=True,
    )
    down_wgrad = jnp.dot(hidden.T, rows_grad, preferred_element_type=jnp.float32).astype(
        jnp.bfloat16
    )
    gate_wgrad = jnp.dot(rows_x.T, gate_grad, preferred_element_type=jnp.float32).astype(
        jnp.bfloat16
    )
    up_wgrad = jnp.dot(rows_x.T, up_grad, preferred_element_type=jnp.float32).astype(jnp.bfloat16)
    back_rows = returned.reshape(slot_count, model_width)
    pair_rows = back_rows[slot_key].reshape(tok_rows, top_count, model_width)
    input_grad = jnp.sum(pair_rows.astype(jnp.float32), axis=1).astype(jnp.bfloat16)
    return (input_grad, gate_wgrad[None], up_wgrad[None], down_wgrad[None])

F32 = jnp.float32
BF16 = jnp.bfloat16
MESH = pl.DeviceIdType.MESH
UP, DOWN, ACROSS, BESIDE = 0, 1, 2, 3


def dense_kernel(
    x_hbm, g_hbm, s_hbm, gw_hbm, uw_hbm, dw_hbm,
    ig_ref, gg_ref, ug_ref, dg_ref,
    xs, gs, ss, w, wd, gu, ht, rc, rp, rb, ra, ru, rd,
    load_sem, send_sem, recv_sem, rb_send, rb_recv, ra_send, ra_recv, ru_send, ru_recv,
    rd_send, rd_recv,
):
    rep, grp, mem = lax.axis_index("rep"), lax.axis_index("grp"), lax.axis_index("mem")
    groups = lax.axis_size("grp")
    cores = lax.axis_size("mem")
    rows = x_hbm.shape[0]
    width = x_hbm.shape[1]
    ff = gw_hbm.shape[1]
    experts = s_hbm.shape[0]
    length = groups // 2
    z, y = grp // 2, grp % 2
    me = grp * cores + mem
    peers = {
        UP: (rep, (z + 1) * 2 + y, mem),
        DOWN: (rep, (z - 1) * 2 + y, mem),
        ACROSS: (rep, z * 2 + 1 - y, mem),
        BESIDE: (rep, grp, 1 - mem),
    }
    has_up, has_down = z < length - 1, z > 0

    def slot(g, c, size):
        return pl.ds(pl.multiple_of((g * cores + c) * size, size), size)

    sizes = (rows, rows, experts)
    bufs = (xs, gs, ss)
    loads = [
        pltpu.make_async_copy(h, b.at[slot(grp, mem, n)], load_sem.at[i])
        for i, (h, b, n) in enumerate(zip((x_hbm, g_hbm, s_hbm), bufs, sizes))
    ]
    loads.append(pltpu.make_async_copy(gw_hbm, w.at[:, pl.ds(0, ff)], load_sem.at[3]))
    loads.append(pltpu.make_async_copy(uw_hbm, w.at[:, pl.ds(ff, ff)], load_sem.at[4]))
    loads.append(pltpu.make_async_copy(dw_hbm, wd, load_sem.at[5]))
    for load in loads:
        load.start()

    barrier = pltpu.get_barrier_semaphore()
    for way, there in ((UP, has_up), (DOWN, has_down), (ACROSS, None), (BESIDE, None)):

        def hail(way=way):
            pl.semaphore_signal(barrier, inc=1, device_id=peers[way], device_id_type=MESH)

        hail() if there is None else pl.when(there)(hail)
    pl.semaphore_wait(barrier, 2 + jnp.where(has_up, 1, 0) + jnp.where(has_down, 1, 0))

    for load in loads[:3]:
        load.wait()

    def hop(way, a, g, c):
        ref = bufs[a].at[slot(g, c, sizes[a])]
        return pltpu.make_async_remote_copy(
            src_ref=ref,
            dst_ref=ref,
            send_sem=send_sem.at[way, a, g],
            recv_sem=recv_sem.at[a, g * cores + c],
            device_id=peers[way],
            device_id_type=MESH,
        )

    def beside(g):
        return pltpu.make_async_remote_copy(
            src_ref=rp.at[slot(g, 1 - mem, rows)],
            dst_ref=rb.at[pl.ds(pl.multiple_of(g * rows, rows), rows)],
            send_sem=rb_send.at[g],
            recv_sem=rb_recv.at[g],
            device_id=peers[BESIDE],
            device_id_type=MESH,
        )

    def line(way, d):
        buf, snd, rcv = {
            UP: (ru, ru_send, ru_recv),
            DOWN: (rd, rd_send, rd_recv),
            ACROSS: (ra, ra_send, ra_recv),
        }[way]
        row = 1 - y if way == ACROSS else y
        return pltpu.make_async_remote_copy(
            src_ref=rp.at[slot(d * 2 + row, mem, rows)],
            dst_ref=buf.at[pl.ds(pl.multiple_of(d * rows, rows), rows)],
            send_sem=snd.at[d],
            recv_sem=rcv.at[d],
            device_id=peers[way],
            device_id_type=MESH,
        )

    def add_into(g, buf, b):
        step = 16

        @pl.loop(0, rows // step)
        def _(i):
            at = pl.ds(pl.multiple_of((g * cores + mem) * rows + i * step, step), step)
            other = pl.ds(pl.multiple_of(b * rows + i * step, step), step)
            rp[at, :] = (rp[at, :].astype(F32) + buf[other, :].astype(F32)).astype(BF16)

    def place(q):
        s = (q + 1) // 2
        sign = 1 - 2 * (q % 2)
        oz = z + sign * s
        return oz, (q >= 0) & (q < 2 * length - 1) & (oz >= 0) & (oz < length)

    def along(p):
        oz, valid = place(p)
        g = oz * 2 + y

        @pl.when(valid)
        def _():
            for a in (2, 0, 1):

                @pl.when(p > 0)
                def _():
                    hop(UP, a, g, mem).wait_recv()

                @pl.when((oz <= z) & has_up)
                def _():
                    hop(UP, a, g, mem).start()

                @pl.when((oz >= z) & has_down)
                def _():
                    hop(DOWN, a, g, mem).start()

                hop(ACROSS, a, g, mem).start()
                hop(BESIDE, a, g, mem).start()

    def across(q):
        oz, valid = place(q)
        g = oz * 2 + 1 - y

        @pl.when(valid)
        def _():
            for a in (2, 0, 1):
                hop(ACROSS, a, g, mem).wait_recv()
                hop(BESIDE, a, g, mem).start()

    def merge(q, row):
        oz, valid = place(q)
        g = oz * 2 + row

        @pl.when(valid)
        def _():
            beside(g).wait_recv()
            add_into(g, rb, g)

            @pl.when(row != y)
            def _():
                line(ACROSS, oz).start()

    def chunk(g):
        for a in (2, 0, 1):
            hop(BESIDE, a, g, 1 - mem).wait_recv()
        block = pl.ds(pl.multiple_of(g * cores * rows, cores * rows), cores * rows)
        ratios = []
        for c in range(cores):
            share = ss[slot(g, c, experts), :]
            picked = lax.broadcasted_iota(jnp.int32, share.shape, 0) == me
            row = jnp.sum(jnp.where(picked, share, 0.0), axis=0, keepdims=True)
            square = jnp.broadcast_to(row, (rows, rows))
            diagonal = lax.broadcasted_iota(jnp.int32, (rows, rows), 0) == (
                lax.broadcasted_iota(jnp.int32, (rows, rows), 1)
            )
            ratios.append(jnp.sum(jnp.where(diagonal, square, 0.0), axis=1, keepdims=True))
        ratio = jnp.concatenate(ratios, axis=0)
        rc[block, :] = ratio
        pre = jnp.dot(xs[block, :], w[...], preferred_element_type=F32)
        gate_pre, up_pre = pre[:, :ff], pre[:, ff:]
        sg = (ratio * gs[block, :].astype(F32)).astype(BF16)
        hidden_grad = lax.dot_general(
            sg, wd[...], (((1,), (1,)), ((), ())), preferred_element_type=F32
        )
        sig = jax.nn.sigmoid(gate_pre)
        act = gate_pre * sig
        ht[:, block] = (act * up_pre).T.astype(BF16)
        gate_grad = (hidden_grad * up_pre * sig * (1.0 + gate_pre * (1.0 - sig))).astype(BF16)
        up_grad = (hidden_grad * act).astype(BF16)
        gu[block, pl.ds(0, ff)] = gate_grad
        gu[block, pl.ds(ff, ff)] = up_grad
        both = jnp.concatenate([gate_grad, up_grad], axis=1)
        rp[block, :] = lax.dot_general(
            both, w[...], (((1,), (1,)), ((), ())), preferred_element_type=F32
        ).astype(BF16)
        beside(g).start()

    @pl.loop(0, 2 * length + 1)
    def _(p):
        along(p)
        across(p - 1)

        @pl.when(p == 0)
        def _():
            for load in loads[3:]:
                load.wait()

        @pl.loop(0, 2)
        def _(j):
            merge(p - 2 + j, jnp.where(j == 0, 1 - y, y))

        @pl.loop(0, 2)
        def _(j):
            oz, valid = place(p - 1 + j)

            @pl.when(valid)
            def _():
                chunk(oz * 2 + jnp.where(j == 0, 1 - y, y))

    def gather_across(d):
        line(ACROSS, d).wait_recv()
        add_into(d * 2 + y, ra, d)

    tile = width // (2 * length)

    @pl.loop(0, length)
    def _(i):
        d = length - 1 - i

        @pl.when(d > z)
        def _():
            gather_across(d)

            @pl.when(has_down)
            def _():
                line(UP, d).wait_recv()
                add_into(d * 2 + y, ru, d)

            line(UP, d).start()

        @pl.when(i < z)
        def _():
            gather_across(i)

            @pl.when(has_up)
            def _():
                line(DOWN, i).wait_recv()
                add_into(i * 2 + y, rd, i)

            line(DOWN, i).start()

        @pl.loop(0, 2)
        def _(t):
            cols = pl.ds(pl.multiple_of((i * 2 + t) * tile, tile), tile)
            wide = lax.dot_general(
                xs[:, cols], gu[...], (((0,), (0,)), ((), ())), preferred_element_type=F32
            ).astype(BF16)
            gg_ref[cols, :] = wide[:, :ff]
            ug_ref[cols, :] = wide[:, ff:]
            sg = (rc[...] * gs[:, cols].astype(F32)).astype(BF16)
            dg_ref[:, cols] = jnp.dot(ht[...], sg, preferred_element_type=F32).astype(BF16)

    gather_across(z)

    @pl.when(has_down)
    def _():
        line(UP, z).wait_recv()
        add_into(grp, ru, z)

    @pl.when(has_up)
    def _():
        line(DOWN, z).wait_recv()
        add_into(grp, rd, z)

    ig_ref[...] = rp[slot(grp, mem, rows), :]

    @pl.loop(0, groups)
    def _(g):
        for a in range(3):
            hop(BESIDE, a, g, mem).wait_send()
        beside(g).wait_send()

    @pl.loop(0, length)
    def _(d):
        g = d * 2 + y
        for a in range(3):
            hop(ACROSS, a, g, mem).wait_send()

            @pl.when((d <= z) & has_up)
            def _():
                hop(UP, a, g, mem).wait_send()

            @pl.when((d >= z) & has_down)
            def _():
                hop(DOWN, a, g, mem).wait_send()

        line(ACROSS, d).wait_send()

        @pl.when(d > z)
        def _():
            line(UP, d).wait_send()

        @pl.when(d < z)
        def _():
            line(DOWN, d).wait_send()


def dense(layer_input, output_grad, expert_ids, route_ints, w_gate, w_up, w_down):
    groups, cores = lax.axis_size("grp"), lax.axis_size("mem")
    devices = groups * cores
    length = groups // 2
    tok_rows, width = layer_input.shape
    ff = w_gate.shape[2]
    total = devices * tok_rows
    quotas = route_ints.astype(F32)
    route_ratio = quotas / jnp.sum(quotas, axis=1, keepdims=True)
    experts = jnp.arange(devices, dtype=jnp.int32)
    share = jnp.sum(
        jnp.where(
            expert_ids.T[None, :, :] == experts[:, None, None], route_ratio.T[None, :, :], 0.0
        ),
        axis=1,
    )
    dma = pltpu.SemaphoreType.DMA
    outs = pl.pallas_call(
        dense_kernel,
        out_shape=(
            jax.ShapeDtypeStruct((tok_rows, width), BF16),
            jax.ShapeDtypeStruct((width, ff), BF16),
            jax.ShapeDtypeStruct((width, ff), BF16),
            jax.ShapeDtypeStruct((ff, width), BF16),
        ),
        in_specs=[pl.BlockSpec(memory_space=pl.ANY)] * 6,
        out_specs=tuple([pl.BlockSpec(memory_space=pltpu.VMEM)] * 4),
        scratch_shapes=[
            pltpu.VMEM((total, width), BF16),
            pltpu.VMEM((total, width), BF16),
            pltpu.VMEM((devices * devices, tok_rows), F32),
            pltpu.VMEM((width, 2 * ff), BF16),
            pltpu.VMEM((ff, width), BF16),
            pltpu.VMEM((total, 2 * ff), BF16),
            pltpu.VMEM((ff, total), BF16),
            pltpu.VMEM((total, 1), F32),
            pltpu.VMEM((total, width), BF16),
            pltpu.VMEM((groups * tok_rows, width), BF16),
            pltpu.VMEM((length * tok_rows, width), BF16),
            pltpu.VMEM((length * tok_rows, width), BF16),
            pltpu.VMEM((length * tok_rows, width), BF16),
            dma((6,)),
            dma((4, 3, groups)),
            dma((3, devices)),
            dma((groups,)),
            dma((groups,)),
            dma((length,)),
            dma((length,)),
            dma((length,)),
            dma((length,)),
            dma((length,)),
            dma((length,)),
        ],
        compiler_params=pltpu.CompilerParams(
            collective_id=0, has_side_effects=True, vmem_limit_bytes=60 * 1024 * 1024
        ),
        cost_estimate=pl.CostEstimate(
            flops=16 * total * width * ff,
            bytes_accessed=12 * width * ff + 6 * tok_rows * width,
            transcendentals=total * ff,
        ),
    )(layer_input, output_grad, share, w_gate[0], w_up[0], w_down[0])
    return (outs[0], outs[1][None], outs[2][None], outs[3][None])


def local(layer_input, output_grad, expert_ids, *rest):
    groups, cores = lax.axis_size("grp"), lax.axis_size("mem")
    tok_rows, top_count = expert_ids.shape
    capacity = max(2, 9 * tok_rows * top_count // (8 * groups * cores))
    suits = tok_rows <= 2 * capacity and groups % 2 == 0 and cores == 2
    plan = dense if suits else routed
    return plan(layer_input, output_grad, expert_ids, *rest)


def solution(mesh):
    return jax.shard_map(
        local,
        mesh=mesh,
        in_specs=(
            P(("rep", "grp", "mem"), None),
            P(("rep", "grp", "mem"), None),
            P(("rep", "grp", "mem"), None),
            P(("rep", "grp", "mem"), None),
            P(("grp", "mem"), None, None),
            P(("grp", "mem"), None, None),
            P(("grp", "mem"), None, None),
        ),
        out_specs=(
            P(("rep", "grp", "mem"), None),
            P(("rep", "grp", "mem"), None, None),
            P(("rep", "grp", "mem"), None, None),
            P(("rep", "grp", "mem"), None, None),
        ),
        check_vma=False,
    )
```

```python
import jax
import jax.numpy as jnp
from jax import lax
from jax.experimental import pallas as pl
from jax.experimental.pallas import tpu as pltpu
from jax.sharding import PartitionSpec as P


def routed(layer_input, output_grad, expert_ids, route_ints, w_gate, w_up, w_down):
    devices = lax.axis_size("grp") * lax.axis_size("mem")
    tok_rows = layer_input.shape[0]
    model_width = layer_input.shape[1]
    top_count = expert_ids.shape[1]
    pair_count = tok_rows * top_count
    capacity = max(2, 9 * tok_rows * top_count // (8 * devices))
    slot_count = devices * capacity
    quotas = route_ints.astype(jnp.float32)
    route_ratio = quotas / jnp.sum(quotas, axis=1, keepdims=True)
    scaled = (route_ratio[:, :, None] * output_grad.astype(jnp.float32)[:, None, :]).astype(
        jnp.bfloat16
    )
    scaled = scaled.reshape(pair_count, model_width)
    flat_ids = expert_ids.reshape(pair_count)
    pair_order = jnp.arange(pair_count, dtype=jnp.int32)
    earlier = (flat_ids[None, :] == flat_ids[:, None]) & (pair_order[None, :] < pair_order[:, None])
    slot_rank = jnp.sum(earlier.astype(jnp.int32), axis=1)
    slot_key = flat_ids * capacity + slot_rank
    slot_match = slot_key[None, :] == jnp.arange(slot_count, dtype=jnp.int32)[:, None]
    filled = jnp.any(slot_match, axis=1)
    source_pair = jnp.sum(jnp.where(slot_match, pair_order[None, :], 0), axis=1)
    send_x = jnp.where(
        filled[:, None], layer_input[source_pair // top_count], jnp.zeros((), jnp.bfloat16)
    )
    send_grad = jnp.where(filled[:, None], scaled[source_pair], jnp.zeros((), jnp.bfloat16))
    recv_x, recv_grad = (
        lax.all_to_all(
            send_x.reshape(devices, capacity, model_width),
            ("grp", "mem"),
            split_axis=0,
            concat_axis=0,
            tiled=True,
        ),
        lax.all_to_all(
            send_grad.reshape(devices, capacity, model_width),
            ("grp", "mem"),
            split_axis=0,
            concat_axis=0,
            tiled=True,
        ),
    )
    rows_x = recv_x.reshape(slot_count, model_width)
    rows_grad = recv_grad.reshape(slot_count, model_width)
    gate_w = w_gate[0]
    up_w = w_up[0]
    down_w = w_down[0]
    gate_pre = jnp.dot(rows_x, gate_w, preferred_element_type=jnp.float32)
    up_pre = jnp.dot(rows_x, up_w, preferred_element_type=jnp.float32)
    sigmoid_gate = jax.nn.sigmoid(gate_pre)
    activity = gate_pre * sigmoid_gate
    hidden = (activity * up_pre).astype(jnp.bfloat16)
    hidden_grad = jnp.dot(rows_grad, down_w.T, preferred_element_type=jnp.float32)
    up_grad = (hidden_grad * activity).astype(jnp.bfloat16)
    gate_grad = (
        hidden_grad * up_pre * sigmoid_gate * (1.0 + gate_pre * (1.0 - sigmoid_gate))
    ).astype(jnp.bfloat16)
    row_grad = (
        jnp.dot(gate_grad, gate_w.T, preferred_element_type=jnp.float32)
        + jnp.dot(up_grad, up_w.T, preferred_element_type=jnp.float32)
    ).astype(jnp.bfloat16)
    returned = lax.all_to_all(
        row_grad.reshape(devices, capacity, model_width),
        ("grp", "mem"),
        split_axis=0,
        concat_axis=0,
        tiled=True,
    )
    down_wgrad = jnp.dot(hidden.T, rows_grad, preferred_element_type=jnp.float32).astype(
        jnp.bfloat16
    )
    gate_wgrad = jnp.dot(rows_x.T, gate_grad, preferred_element_type=jnp.float32).astype(
        jnp.bfloat16
    )
    up_wgrad = jnp.dot(rows_x.T, up_grad, preferred_element_type=jnp.float32).astype(jnp.bfloat16)
    back_rows = returned.reshape(slot_count, model_width)
    pair_rows = back_rows[slot_key].reshape(tok_rows, top_count, model_width)
    input_grad = jnp.sum(pair_rows.astype(jnp.float32), axis=1).astype(jnp.bfloat16)
    return (input_grad, gate_wgrad[None], up_wgrad[None], down_wgrad[None])

F32 = jnp.float32
BF16 = jnp.bfloat16
MESH = pl.DeviceIdType.MESH
UP, DOWN, ACROSS, BESIDE = 0, 1, 2, 3


def dense_kernel(
    x_hbm, g_hbm, s_hbm, gw_hbm, uw_hbm, dw_hbm,
    ig_ref, gg_ref, ug_ref, dg_ref,
    xs, gs, ss, w, wd, gu, ht, rc, rp, rb, ra, ru, rd,
    load_sem, send_sem, recv_sem, rb_send, rb_recv, ra_send, ra_recv, ru_send, ru_recv,
    rd_send, rd_recv,
):
    rep, grp, mem = lax.axis_index("rep"), lax.axis_index("grp"), lax.axis_index("mem")
    groups = lax.axis_size("grp")
    cores = lax.axis_size("mem")
    rows = x_hbm.shape[0]
    width = x_hbm.shape[1]
    ff = gw_hbm.shape[1]
    experts = s_hbm.shape[0]
    length = groups // 2
    z, y = grp // 2, grp % 2
    me = grp * cores + mem
    peers = {
        UP: (rep, (z + 1) * 2 + y, mem),
        DOWN: (rep, (z - 1) * 2 + y, mem),
        ACROSS: (rep, z * 2 + 1 - y, mem),
        BESIDE: (rep, grp, 1 - mem),
    }
    has_up, has_down = z < length - 1, z > 0

    def slot(g, c, size):
        return pl.ds(pl.multiple_of((g * cores + c) * size, size), size)

    sizes = (rows, rows, experts)
    bufs = (xs, gs, ss)
    loads = [
        pltpu.make_async_copy(h, b.at[slot(grp, mem, n)], load_sem.at[i])
        for i, (h, b, n) in enumerate(zip((x_hbm, g_hbm, s_hbm), bufs, sizes))
    ]
    loads.append(pltpu.make_async_copy(gw_hbm, w.at[:, pl.ds(0, ff)], load_sem.at[3]))
    loads.append(pltpu.make_async_copy(uw_hbm, w.at[:, pl.ds(ff, ff)], load_sem.at[4]))
    loads.append(pltpu.make_async_copy(dw_hbm, wd, load_sem.at[5]))
    for load in loads:
        load.start()

    barrier = pltpu.get_barrier_semaphore()
    for way, there in ((UP, has_up), (DOWN, has_down), (ACROSS, None), (BESIDE, None)):

        def hail(way=way):
            pl.semaphore_signal(barrier, inc=1, device_id=peers[way], device_id_type=MESH)

        hail() if there is None else pl.when(there)(hail)
    pl.semaphore_wait(barrier, 2 + jnp.where(has_up, 1, 0) + jnp.where(has_down, 1, 0))

    for load in loads[:3]:
        load.wait()

    def hop(way, a, g, c):
        ref = bufs[a].at[slot(g, c, sizes[a])]
        return pltpu.make_async_remote_copy(
            src_ref=ref,
            dst_ref=ref,
            send_sem=send_sem.at[way, a, g],
            recv_sem=recv_sem.at[a, g * cores + c],
            device_id=peers[way],
            device_id_type=MESH,
        )

    def beside(g):
        return pltpu.make_async_remote_copy(
            src_ref=rp.at[slot(g, 1 - mem, rows)],
            dst_ref=rb.at[pl.ds(pl.multiple_of(g * rows, rows), rows)],
            send_sem=rb_send.at[g],
            recv_sem=rb_recv.at[g],
            device_id=peers[BESIDE],
            device_id_type=MESH,
        )

    half = rows // 2

    def line(way, g, h):
        buf, snd, rcv = {
            UP: (ru, ru_send, ru_recv),
            DOWN: (rd, rd_send, rd_recv),
            ACROSS: (ra, ra_send, ra_recv),
        }[way]
        at = 0 if way == ACROSS else g
        return pltpu.make_async_remote_copy(
            src_ref=rp.at[pl.ds(pl.multiple_of((g * cores + mem) * rows + h * half, half), half)],
            dst_ref=buf.at[pl.ds(pl.multiple_of(at * rows + h * half, half), half)],
            send_sem=snd.at[at, h],
            recv_sem=rcv.at[at, h],
            device_id=peers[way],
            device_id_type=MESH,
        )

    def add_into(g, buf, b, h):
        step = 16

        @pl.loop(0, half // step)
        def _(i):
            shift = h * half + i * step
            at = pl.ds(pl.multiple_of((g * cores + mem) * rows + shift, step), step)
            other = pl.ds(pl.multiple_of(b * rows + shift, step), step)
            rp[at, :] = (rp[at, :].astype(F32) + buf[other, :].astype(F32)).astype(BF16)

    def place(q):
        s = (q + 1) // 2
        sign = 1 - 2 * (q % 2)
        oz = z + sign * s
        return oz, (q >= 0) & (q < 2 * length - 1) & (oz >= 0) & (oz < length)

    def along(p, arrays):
        oz, valid = place(p)
        g = oz * 2 + y

        @pl.when(valid)
        def _():
            for a in arrays:

                @pl.when(p > 0)
                def _():
                    hop(UP, a, g, mem).wait_recv()

                @pl.when((oz <= z) & has_up)
                def _():
                    hop(UP, a, g, mem).start()

                @pl.when((oz >= z) & has_down)
                def _():
                    hop(DOWN, a, g, mem).start()

                hop(ACROSS, a, g, mem).start()
                hop(BESIDE, a, g, mem).start()

    def across(q):
        oz, valid = place(q)
        g = oz * 2 + 1 - y

        @pl.when(valid)
        def _():
            for a in (2, 0, 1):
                hop(ACROSS, a, g, mem).wait_recv()
                hop(BESIDE, a, g, mem).start()

    def merge(q, row):
        oz, valid = place(q)
        g = oz * 2 + row

        @pl.when(valid)
        def _():
            beside(g).wait_recv()

            @pl.loop(0, 2)
            def _(h):
                add_into(g, rb, g, h)

                @pl.when((oz > z) & ~has_down)
                def _():
                    line(UP, g, h).start()

                @pl.when((oz < z) & ~has_up)
                def _():
                    line(DOWN, g, h).start()

    def chunk(g):
        for a in (2, 0, 1):
            hop(BESIDE, a, g, 1 - mem).wait_recv()
        block = pl.ds(pl.multiple_of(g * cores * rows, cores * rows), cores * rows)
        ratios = []
        for c in range(cores):
            share = ss[slot(g, c, experts), :]
            picked = lax.broadcasted_iota(jnp.int32, share.shape, 0) == me
            row = jnp.sum(jnp.where(picked, share, 0.0), axis=0, keepdims=True)
            square = jnp.broadcast_to(row, (rows, rows))
            diagonal = lax.broadcasted_iota(jnp.int32, (rows, rows), 0) == (
                lax.broadcasted_iota(jnp.int32, (rows, rows), 1)
            )
            ratios.append(jnp.sum(jnp.where(diagonal, square, 0.0), axis=1, keepdims=True))
        ratio = jnp.concatenate(ratios, axis=0)
        rc[block, :] = ratio
        pre = jnp.dot(xs[block, :], w[...], preferred_element_type=F32)
        gate_pre, up_pre = pre[:, :ff], pre[:, ff:]
        sg = (ratio * gs[block, :].astype(F32)).astype(BF16)
        hidden_grad = lax.dot_general(
            sg, wd[...], (((1,), (1,)), ((), ())), preferred_element_type=F32
        )
        sig = jax.nn.sigmoid(gate_pre)
        act = gate_pre * sig
        ht[:, block] = (act * up_pre).T.astype(BF16)
        gate_grad = (hidden_grad * up_pre * sig * (1.0 + gate_pre * (1.0 - sig))).astype(BF16)
        up_grad = (hidden_grad * act).astype(BF16)
        gu[block, pl.ds(0, ff)] = gate_grad
        gu[block, pl.ds(ff, ff)] = up_grad
        both = jnp.concatenate([gate_grad, up_grad], axis=1)
        rp[block, :] = lax.dot_general(
            both, w[...], (((1,), (1,)), ((), ())), preferred_element_type=F32
        ).astype(BF16)
        beside(g).start()

    def ahead(p, arrays):
        @pl.loop(0, 2)
        def _(k):
            @pl.when((p % 2 == 1) | (p + k == 0))
            def _():
                along(p + k, arrays)

    @pl.loop(0, 2 * length + 1)
    def _(p):
        @pl.loop(0, 2)
        def _(j):
            @pl.when(j == 0)
            def _():
                ahead(p, (2, 0))
                across(p - 1)

                @pl.loop(0, 2)
                def _(k):
                    merge(p - 2 + k, jnp.where(k == 0, 1 - y, y))

            @pl.when(j == 1)
            def _():
                ahead(p, (1,))

                @pl.when(p == 0)
                def _():
                    for load in loads[3:]:
                        load.wait()

            oz, valid = place(p - 1 + j)

            @pl.when(valid)
            def _():
                chunk(oz * 2 + jnp.where(j == 0, 1 - y, y))

    def relay(level, near):
        up, down = near, length - 1 - near

        @pl.loop(0, 4)
        def _(k):
            row = jnp.where(k < 2, y, 1 - y)
            h = k % 2

            @pl.when((z == level) & (up > z))
            def _():
                g = up * 2 + row
                line(UP, g, h).wait_recv()
                add_into(g, ru, g, h)
                line(UP, g, h).start()

            @pl.when((length - 1 - z == level) & (down < z))
            def _():
                g = down * 2 + row
                line(DOWN, g, h).wait_recv()
                add_into(g, rd, g, h)
                line(DOWN, g, h).start()

    tile = width // (2 * length)

    @pl.loop(0, max(2 * length, (length - 1) * length))
    def _(t):
        @pl.when(t < 2 * length)
        def _():
            cols = pl.ds(pl.multiple_of(t * tile, tile), tile)
            wide = lax.dot_general(
                xs[:, cols], gu[...], (((0,), (0,)), ((), ())), preferred_element_type=F32
            ).astype(BF16)
            gg_ref[cols, :] = wide[:, :ff]
            ug_ref[cols, :] = wide[:, ff:]
            sg = (rc[...] * gs[:, cols].astype(F32)).astype(BF16)
            dg_ref[:, cols] = jnp.dot(ht[...], sg, preferred_element_type=F32).astype(BF16)

        relay(1 + t // length, t % length)

    @pl.loop(0, 4)
    def _(k):
        g = z * 2 + jnp.where(k < 2, 1 - y, y)
        h = k % 2

        @pl.when(has_down)
        def _():
            line(UP, g, h).wait_recv()
            add_into(g, ru, g, h)

        @pl.when(has_up)
        def _():
            line(DOWN, g, h).wait_recv()
            add_into(g, rd, g, h)

        @pl.when(k < 2)
        def _():
            line(ACROSS, g, h).start()

    @pl.loop(0, 2)
    def _(h):
        line(ACROSS, grp, h).wait_recv()
        add_into(grp, ra, 0, h)

    ig_ref[...] = rp[slot(grp, mem, rows), :]

    @pl.loop(0, groups)
    def _(g):
        for a in range(3):
            hop(BESIDE, a, g, mem).wait_send()
        beside(g).wait_send()

    @pl.loop(0, length)
    def _(d):
        g = d * 2 + y
        for a in range(3):
            hop(ACROSS, a, g, mem).wait_send()

            @pl.when((d <= z) & has_up)
            def _():
                hop(UP, a, g, mem).wait_send()

            @pl.when((d >= z) & has_down)
            def _():
                hop(DOWN, a, g, mem).wait_send()

        @pl.loop(0, 4)
        def _(k):
            @pl.when(d > z)
            def _():
                line(UP, d * 2 + k // 2, k % 2).wait_send()

            @pl.when(d < z)
            def _():
                line(DOWN, d * 2 + k // 2, k % 2).wait_send()

    @pl.loop(0, 2)
    def _(h):
        line(ACROSS, z * 2 + 1 - y, h).wait_send()


def dense(layer_input, output_grad, expert_ids, route_ints, w_gate, w_up, w_down):
    groups, cores = lax.axis_size("grp"), lax.axis_size("mem")
    devices = groups * cores
    length = groups // 2
    tok_rows, width = layer_input.shape
    ff = w_gate.shape[2]
    total = devices * tok_rows
    quotas = route_ints.astype(F32)
    route_ratio = quotas / jnp.sum(quotas, axis=1, keepdims=True)
    experts = jnp.arange(devices, dtype=jnp.int32)
    share = jnp.sum(
        jnp.where(
            expert_ids.T[None, :, :] == experts[:, None, None], route_ratio.T[None, :, :], 0.0
        ),
        axis=1,
    )
    dma = pltpu.SemaphoreType.DMA
    outs = pl.pallas_call(
        dense_kernel,
        out_shape=(
            jax.ShapeDtypeStruct((tok_rows, width), BF16),
            jax.ShapeDtypeStruct((width, ff), BF16),
            jax.ShapeDtypeStruct((width, ff), BF16),
            jax.ShapeDtypeStruct((ff, width), BF16),
        ),
        in_specs=[pl.BlockSpec(memory_space=pl.ANY)] * 6,
        out_specs=tuple([pl.BlockSpec(memory_space=pltpu.VMEM)] * 4),
        scratch_shapes=[
            pltpu.VMEM((total, width), BF16),
            pltpu.VMEM((total, width), BF16),
            pltpu.VMEM((devices * devices, tok_rows), F32),
            pltpu.VMEM((width, 2 * ff), BF16),
            pltpu.VMEM((ff, width), BF16),
            pltpu.VMEM((total, 2 * ff), BF16),
            pltpu.VMEM((ff, total), BF16),
            pltpu.VMEM((total, 1), F32),
            pltpu.VMEM((total, width), BF16),
            pltpu.VMEM((groups * tok_rows, width), BF16),
            pltpu.VMEM((tok_rows, width), BF16),
            pltpu.VMEM((groups * tok_rows, width), BF16),
            pltpu.VMEM((groups * tok_rows, width), BF16),
            dma((6,)),
            dma((4, 3, groups)),
            dma((3, devices)),
            dma((groups,)),
            dma((groups,)),
            dma((1, 2)),
            dma((1, 2)),
            dma((groups, 2)),
            dma((groups, 2)),
            dma((groups, 2)),
            dma((groups, 2)),
        ],
        compiler_params=pltpu.CompilerParams(
            collective_id=0, has_side_effects=True, vmem_limit_bytes=60 * 1024 * 1024
        ),
        cost_estimate=pl.CostEstimate(
            flops=16 * total * width * ff,
            bytes_accessed=12 * width * ff + 6 * tok_rows * width,
            transcendentals=total * ff,
        ),
    )(layer_input, output_grad, share, w_gate[0], w_up[0], w_down[0])
    return (outs[0], outs[1][None], outs[2][None], outs[3][None])


def local(layer_input, output_grad, expert_ids, *rest):
    groups, cores = lax.axis_size("grp"), lax.axis_size("mem")
    tok_rows, top_count = expert_ids.shape
    capacity = max(2, 9 * tok_rows * top_count // (8 * groups * cores))
    suits = tok_rows <= 2 * capacity and groups % 2 == 0 and cores == 2
    plan = dense if suits else routed
    return plan(layer_input, output_grad, expert_ids, *rest)


def solution(mesh):
    return jax.shard_map(
        local,
        mesh=mesh,
        in_specs=(
            P(("rep", "grp", "mem"), None),
            P(("rep", "grp", "mem"), None),
            P(("rep", "grp", "mem"), None),
            P(("rep", "grp", "mem"), None),
            P(("grp", "mem"), None, None),
            P(("grp", "mem"), None, None),
            P(("grp", "mem"), None, None),
        ),
        out_specs=(
            P(("rep", "grp", "mem"), None),
            P(("rep", "grp", "mem"), None, None),
            P(("rep", "grp", "mem"), None, None),
            P(("rep", "grp", "mem"), None, None),
        ),
        check_vma=False,
    )
```

```python
import jax
import jax.numpy as jnp
from jax import lax
from jax.experimental import pallas as pl
from jax.experimental.pallas import tpu as pltpu
from jax.sharding import PartitionSpec as P


def routed(layer_input, output_grad, expert_ids, route_ints, w_gate, w_up, w_down):
    devices = lax.axis_size("grp") * lax.axis_size("mem")
    tok_rows = layer_input.shape[0]
    model_width = layer_input.shape[1]
    top_count = expert_ids.shape[1]
    pair_count = tok_rows * top_count
    capacity = max(2, 9 * tok_rows * top_count // (8 * devices))
    slot_count = devices * capacity
    quotas = route_ints.astype(jnp.float32)
    route_ratio = quotas / jnp.sum(quotas, axis=1, keepdims=True)
    scaled = (route_ratio[:, :, None] * output_grad.astype(jnp.float32)[:, None, :]).astype(
        jnp.bfloat16
    )
    scaled = scaled.reshape(pair_count, model_width)
    flat_ids = expert_ids.reshape(pair_count)
    pair_order = jnp.arange(pair_count, dtype=jnp.int32)
    earlier = (flat_ids[None, :] == flat_ids[:, None]) & (pair_order[None, :] < pair_order[:, None])
    slot_rank = jnp.sum(earlier.astype(jnp.int32), axis=1)
    slot_key = flat_ids * capacity + slot_rank
    slot_match = slot_key[None, :] == jnp.arange(slot_count, dtype=jnp.int32)[:, None]
    filled = jnp.any(slot_match, axis=1)
    source_pair = jnp.sum(jnp.where(slot_match, pair_order[None, :], 0), axis=1)
    send_x = jnp.where(
        filled[:, None], layer_input[source_pair // top_count], jnp.zeros((), jnp.bfloat16)
    )
    send_grad = jnp.where(filled[:, None], scaled[source_pair], jnp.zeros((), jnp.bfloat16))
    recv_x, recv_grad = (
        lax.all_to_all(
            send_x.reshape(devices, capacity, model_width),
            ("grp", "mem"),
            split_axis=0,
            concat_axis=0,
            tiled=True,
        ),
        lax.all_to_all(
            send_grad.reshape(devices, capacity, model_width),
            ("grp", "mem"),
            split_axis=0,
            concat_axis=0,
            tiled=True,
        ),
    )
    rows_x = recv_x.reshape(slot_count, model_width)
    rows_grad = recv_grad.reshape(slot_count, model_width)
    gate_w = w_gate[0]
    up_w = w_up[0]
    down_w = w_down[0]
    gate_pre = jnp.dot(rows_x, gate_w, preferred_element_type=jnp.float32)
    up_pre = jnp.dot(rows_x, up_w, preferred_element_type=jnp.float32)
    sigmoid_gate = jax.nn.sigmoid(gate_pre)
    activity = gate_pre * sigmoid_gate
    hidden = (activity * up_pre).astype(jnp.bfloat16)
    hidden_grad = jnp.dot(rows_grad, down_w.T, preferred_element_type=jnp.float32)
    up_grad = (hidden_grad * activity).astype(jnp.bfloat16)
    gate_grad = (
        hidden_grad * up_pre * sigmoid_gate * (1.0 + gate_pre * (1.0 - sigmoid_gate))
    ).astype(jnp.bfloat16)
    row_grad = (
        jnp.dot(gate_grad, gate_w.T, preferred_element_type=jnp.float32)
        + jnp.dot(up_grad, up_w.T, preferred_element_type=jnp.float32)
    ).astype(jnp.bfloat16)
    returned = lax.all_to_all(
        row_grad.reshape(devices, capacity, model_width),
        ("grp", "mem"),
        split_axis=0,
        concat_axis=0,
        tiled=True,
    )
    down_wgrad = jnp.dot(hidden.T, rows_grad, preferred_element_type=jnp.float32).astype(
        jnp.bfloat16
    )
    gate_wgrad = jnp.dot(rows_x.T, gate_grad, preferred_element_type=jnp.float32).astype(
        jnp.bfloat16
    )
    up_wgrad = jnp.dot(rows_x.T, up_grad, preferred_element_type=jnp.float32).astype(jnp.bfloat16)
    back_rows = returned.reshape(slot_count, model_width)
    pair_rows = back_rows[slot_key].reshape(tok_rows, top_count, model_width)
    input_grad = jnp.sum(pair_rows.astype(jnp.float32), axis=1).astype(jnp.bfloat16)
    return (input_grad, gate_wgrad[None], up_wgrad[None], down_wgrad[None])

F32 = jnp.float32
BF16 = jnp.bfloat16
MESH = pl.DeviceIdType.MESH
UP, DOWN, ACROSS, BESIDE = 0, 1, 2, 3


def dense_kernel(
    x_hbm, g_hbm, s_hbm, gw_hbm, uw_hbm, dw_hbm,
    ig_ref, gg_ref, ug_ref, dg_ref,
    xs, gs, ss, w, wd, gu, ht, rc, rp, rb, ra, ru, rd,
    load_sem, send_sem, recv_sem, rb_send, rb_recv, ra_send, ra_recv, ru_send, ru_recv,
    rd_send, rd_recv,
):
    rep, grp, mem = lax.axis_index("rep"), lax.axis_index("grp"), lax.axis_index("mem")
    groups = lax.axis_size("grp")
    cores = lax.axis_size("mem")
    rows = x_hbm.shape[0]
    width = x_hbm.shape[1]
    ff = gw_hbm.shape[1]
    experts = s_hbm.shape[0]
    length = groups // 2
    z, y = grp // 2, grp % 2
    me = grp * cores + mem
    peers = {
        UP: (rep, (z + 1) * 2 + y, mem),
        DOWN: (rep, (z - 1) * 2 + y, mem),
        ACROSS: (rep, z * 2 + 1 - y, mem),
        BESIDE: (rep, grp, 1 - mem),
    }
    has_up, has_down = z < length - 1, z > 0

    def slot(g, c, size):
        return pl.ds(pl.multiple_of((g * cores + c) * size, size), size)

    sizes = (rows, rows, experts)
    bufs = (xs, gs, ss)
    loads = [
        pltpu.make_async_copy(h, b.at[slot(grp, mem, n)], load_sem.at[i])
        for i, (h, b, n) in enumerate(zip((x_hbm, g_hbm, s_hbm), bufs, sizes))
    ]
    loads.append(pltpu.make_async_copy(gw_hbm, w.at[:, pl.ds(0, ff)], load_sem.at[3]))
    loads.append(pltpu.make_async_copy(uw_hbm, w.at[:, pl.ds(ff, ff)], load_sem.at[4]))
    loads.append(pltpu.make_async_copy(dw_hbm, wd, load_sem.at[5]))
    for load in loads:
        load.start()

    barrier = pltpu.get_barrier_semaphore()
    for way, there in ((UP, has_up), (DOWN, has_down), (ACROSS, None), (BESIDE, None)):

        def hail(way=way):
            pl.semaphore_signal(barrier, inc=1, device_id=peers[way], device_id_type=MESH)

        hail() if there is None else pl.when(there)(hail)
    pl.semaphore_wait(barrier, 2 + jnp.where(has_up, 1, 0) + jnp.where(has_down, 1, 0))

    for load in loads[:3]:
        load.wait()

    def hop(way, a, g, c):
        ref = bufs[a].at[slot(g, c, sizes[a])]
        return pltpu.make_async_remote_copy(
            src_ref=ref,
            dst_ref=ref,
            send_sem=send_sem.at[way, a, g],
            recv_sem=recv_sem.at[a, g * cores + c],
            device_id=peers[way],
            device_id_type=MESH,
        )

    def beside(g):
        return pltpu.make_async_remote_copy(
            src_ref=rp.at[slot(g, 1 - mem, rows)],
            dst_ref=rb.at[pl.ds(pl.multiple_of(g * rows, rows), rows)],
            send_sem=rb_send.at[g],
            recv_sem=rb_recv.at[g],
            device_id=peers[BESIDE],
            device_id_type=MESH,
        )

    half = rows // 2

    def line(way, g, h):
        buf, snd, rcv = {
            UP: (ru, ru_send, ru_recv),
            DOWN: (rd, rd_send, rd_recv),
            ACROSS: (ra, ra_send, ra_recv),
        }[way]
        at = 0 if way == ACROSS else g
        return pltpu.make_async_remote_copy(
            src_ref=rp.at[pl.ds(pl.multiple_of((g * cores + mem) * rows + h * half, half), half)],
            dst_ref=buf.at[pl.ds(pl.multiple_of(at * rows + h * half, half), half)],
            send_sem=snd.at[at, h],
            recv_sem=rcv.at[at, h],
            device_id=peers[way],
            device_id_type=MESH,
        )

    def add_into(g, buf, b, h):
        step = 16

        @pl.loop(0, half // step)
        def _(i):
            shift = h * half + i * step
            at = pl.ds(pl.multiple_of((g * cores + mem) * rows + shift, step), step)
            other = pl.ds(pl.multiple_of(b * rows + shift, step), step)
            rp[at, :] = (rp[at, :].astype(F32) + buf[other, :].astype(F32)).astype(BF16)

    def place(q):
        s = (q + 1) // 2
        sign = 1 - 2 * (q % 2)
        oz = z + sign * s
        return oz, (q >= 0) & (q < 2 * length - 1) & (oz >= 0) & (oz < length)

    def along(p, arrays):
        oz, valid = place(p)
        g = oz * 2 + y

        @pl.when(valid)
        def _():
            for a in arrays:

                @pl.when(p > 0)
                def _():
                    hop(UP, a, g, mem).wait_recv()

                @pl.when((oz <= z) & has_up)
                def _():
                    hop(UP, a, g, mem).start()

                @pl.when((oz >= z) & has_down)
                def _():
                    hop(DOWN, a, g, mem).start()

                hop(ACROSS, a, g, mem).start()
                hop(BESIDE, a, g, mem).start()

    def across(q):
        oz, valid = place(q)
        g = oz * 2 + 1 - y

        @pl.when(valid)
        def _():
            for a in (2, 0, 1):
                hop(ACROSS, a, g, mem).wait_recv()
                hop(BESIDE, a, g, mem).start()

    def merge(q, row):
        oz, valid = place(q)
        g = oz * 2 + row

        @pl.when(valid)
        def _():
            beside(g).wait_recv()

            @pl.loop(0, 2)
            def _(h):
                add_into(g, rb, g, h)

                @pl.when((oz > z) & ~has_down)
                def _():
                    line(UP, g, h).start()

                @pl.when((oz < z) & ~has_up)
                def _():
                    line(DOWN, g, h).start()

    def chunk(g):
        for a in (2, 0, 1):
            hop(BESIDE, a, g, 1 - mem).wait_recv()
        block = pl.ds(pl.multiple_of(g * cores * rows, cores * rows), cores * rows)
        ratios = []
        for c in range(cores):
            share = ss[slot(g, c, experts), :]
            picked = lax.broadcasted_iota(jnp.int32, share.shape, 0) == me
            row = jnp.sum(jnp.where(picked, share, 0.0), axis=0, keepdims=True)
            square = jnp.broadcast_to(row, (rows, rows))
            diagonal = lax.broadcasted_iota(jnp.int32, (rows, rows), 0) == (
                lax.broadcasted_iota(jnp.int32, (rows, rows), 1)
            )
            ratios.append(jnp.sum(jnp.where(diagonal, square, 0.0), axis=1, keepdims=True))
        ratio = jnp.concatenate(ratios, axis=0)
        rc[block, :] = ratio
        pre = jnp.dot(xs[block, :], w[...], preferred_element_type=F32)
        gate_pre, up_pre = pre[:, :ff], pre[:, ff:]
        sg = (ratio * gs[block, :].astype(F32)).astype(BF16)
        hidden_grad = lax.dot_general(
            sg, wd[...], (((1,), (1,)), ((), ())), preferred_element_type=F32
        )
        sig = jax.nn.sigmoid(gate_pre)
        act = gate_pre * sig
        ht[:, block] = (act * up_pre).T.astype(BF16)
        gate_grad = (hidden_grad * up_pre * sig * (1.0 + gate_pre * (1.0 - sig))).astype(BF16)
        up_grad = (hidden_grad * act).astype(BF16)
        gu[block, pl.ds(0, ff)] = gate_grad
        gu[block, pl.ds(ff, ff)] = up_grad
        both = jnp.concatenate([gate_grad, up_grad], axis=1)
        rp[block, :] = lax.dot_general(
            both, w[...], (((1,), (1,)), ((), ())), preferred_element_type=F32
        ).astype(BF16)
        beside(g).start()

    def ahead(p, arrays):
        @pl.loop(0, 2)
        def _(k):
            @pl.when((p % 2 == 1) | (p + k == 0))
            def _():
                along(p + k, arrays)

    @pl.loop(0, 2 * length + 1)
    def _(p):
        @pl.loop(0, 2)
        def _(j):
            @pl.when(j == 0)
            def _():
                @pl.loop(0, 2)
                def _(k):
                    merge(p - 2 + k, jnp.where(k == 0, 1 - y, y))

                ahead(p, (2, 0))
                across(p - 1)

            @pl.when(j == 1)
            def _():
                ahead(p, (1,))

                @pl.when(p == 0)
                def _():
                    for load in loads[3:]:
                        load.wait()

            oz, valid = place(p - 1 + j)

            @pl.when(valid)
            def _():
                chunk(oz * 2 + jnp.where(j == 0, 1 - y, y))

    def relay(level, near):
        up, down = near, length - 1 - near

        @pl.loop(0, 4)
        def _(k):
            row = jnp.where(k < 2, y, 1 - y)
            h = k % 2

            @pl.when((z == level) & (up > z))
            def _():
                g = up * 2 + row
                line(UP, g, h).wait_recv()
                add_into(g, ru, g, h)
                line(UP, g, h).start()

            @pl.when((length - 1 - z == level) & (down < z))
            def _():
                g = down * 2 + row
                line(DOWN, g, h).wait_recv()
                add_into(g, rd, g, h)
                line(DOWN, g, h).start()

    tile = width // (2 * length)

    @pl.loop(0, max(2 * length, (length - 1) * length))
    def _(t):
        @pl.when(t < 2 * length)
        def _():
            cols = pl.ds(pl.multiple_of(t * tile, tile), tile)
            wide = lax.dot_general(
                xs[:, cols], gu[...], (((0,), (0,)), ((), ())), preferred_element_type=F32
            ).astype(BF16)
            gg_ref[cols, :] = wide[:, :ff]
            ug_ref[cols, :] = wide[:, ff:]
            sg = (rc[...] * gs[:, cols].astype(F32)).astype(BF16)
            dg_ref[:, cols] = jnp.dot(ht[...], sg, preferred_element_type=F32).astype(BF16)

        relay(1 + t // length, t % length)

    @pl.loop(0, 4)
    def _(k):
        g = z * 2 + jnp.where(k < 2, 1 - y, y)
        h = k % 2

        @pl.when(has_down)
        def _():
            line(UP, g, h).wait_recv()
            add_into(g, ru, g, h)

        @pl.when(has_up)
        def _():
            line(DOWN, g, h).wait_recv()
            add_into(g, rd, g, h)

        @pl.when(k < 2)
        def _():
            line(ACROSS, g, h).start()

    @pl.loop(0, 2)
    def _(h):
        line(ACROSS, grp, h).wait_recv()
        add_into(grp, ra, 0, h)

    ig_ref[...] = rp[slot(grp, mem, rows), :]

    @pl.loop(0, groups)
    def _(g):
        for a in range(3):
            hop(BESIDE, a, g, mem).wait_send()
        beside(g).wait_send()

    @pl.loop(0, length)
    def _(d):
        g = d * 2 + y
        for a in range(3):
            hop(ACROSS, a, g, mem).wait_send()

            @pl.when((d <= z) & has_up)
            def _():
                hop(UP, a, g, mem).wait_send()

            @pl.when((d >= z) & has_down)
            def _():
                hop(DOWN, a, g, mem).wait_send()

        @pl.loop(0, 4)
        def _(k):
            @pl.when(d > z)
            def _():
                line(UP, d * 2 + k // 2, k % 2).wait_send()

            @pl.when(d < z)
            def _():
                line(DOWN, d * 2 + k // 2, k % 2).wait_send()

    @pl.loop(0, 2)
    def _(h):
        line(ACROSS, z * 2 + 1 - y, h).wait_send()


def dense(layer_input, output_grad, expert_ids, route_ints, w_gate, w_up, w_down):
    groups, cores = lax.axis_size("grp"), lax.axis_size("mem")
    devices = groups * cores
    length = groups // 2
    tok_rows, width = layer_input.shape
    ff = w_gate.shape[2]
    total = devices * tok_rows
    quotas = route_ints.astype(F32)
    route_ratio = quotas / jnp.sum(quotas, axis=1, keepdims=True)
    experts = jnp.arange(devices, dtype=jnp.int32)
    share = jnp.sum(
        jnp.where(
            expert_ids.T[None, :, :] == experts[:, None, None], route_ratio.T[None, :, :], 0.0
        ),
        axis=1,
    )
    dma = pltpu.SemaphoreType.DMA
    outs = pl.pallas_call(
        dense_kernel,
        out_shape=(
            jax.ShapeDtypeStruct((tok_rows, width), BF16),
            jax.ShapeDtypeStruct((width, ff), BF16),
            jax.ShapeDtypeStruct((width, ff), BF16),
            jax.ShapeDtypeStruct((ff, width), BF16),
        ),
        in_specs=[pl.BlockSpec(memory_space=pl.ANY)] * 6,
        out_specs=tuple([pl.BlockSpec(memory_space=pltpu.VMEM)] * 4),
        scratch_shapes=[
            pltpu.VMEM((total, width), BF16),
            pltpu.VMEM((total, width), BF16),
            pltpu.VMEM((devices * devices, tok_rows), F32),
            pltpu.VMEM((width, 2 * ff), BF16),
            pltpu.VMEM((ff, width), BF16),
            pltpu.VMEM((total, 2 * ff), BF16),
            pltpu.VMEM((ff, total), BF16),
            pltpu.VMEM((total, 1), F32),
            pltpu.VMEM((total, width), BF16),
            pltpu.VMEM((groups * tok_rows, width), BF16),
            pltpu.VMEM((tok_rows, width), BF16),
            pltpu.VMEM((groups * tok_rows, width), BF16),
            pltpu.VMEM((groups * tok_rows, width), BF16),
            dma((6,)),
            dma((4, 3, groups)),
            dma((3, devices)),
            dma((groups,)),
            dma((groups,)),
            dma((1, 2)),
            dma((1, 2)),
            dma((groups, 2)),
            dma((groups, 2)),
            dma((groups, 2)),
            dma((groups, 2)),
        ],
        compiler_params=pltpu.CompilerParams(
            collective_id=0, has_side_effects=True, vmem_limit_bytes=60 * 1024 * 1024
        ),
        cost_estimate=pl.CostEstimate(
            flops=16 * total * width * ff,
            bytes_accessed=12 * width * ff + 6 * tok_rows * width,
            transcendentals=total * ff,
        ),
    )(layer_input, output_grad, share, w_gate[0], w_up[0], w_down[0])
    return (outs[0], outs[1][None], outs[2][None], outs[3][None])


def local(layer_input, output_grad, expert_ids, *rest):
    groups, cores = lax.axis_size("grp"), lax.axis_size("mem")
    tok_rows, top_count = expert_ids.shape
    capacity = max(2, 9 * tok_rows * top_count // (8 * groups * cores))
    suits = tok_rows <= 2 * capacity and groups % 2 == 0 and cores == 2
    plan = dense if suits else routed
    return plan(layer_input, output_grad, expert_ids, *rest)


def solution(mesh):
    return jax.shard_map(
        local,
        mesh=mesh,
        in_specs=(
            P(("rep", "grp", "mem"), None),
            P(("rep", "grp", "mem"), None),
            P(("rep", "grp", "mem"), None),
            P(("rep", "grp", "mem"), None),
            P(("grp", "mem"), None, None),
            P(("grp", "mem"), None, None),
            P(("grp", "mem"), None, None),
        ),
        out_specs=(
            P(("rep", "grp", "mem"), None),
            P(("rep", "grp", "mem"), None, None),
            P(("rep", "grp", "mem"), None, None),
            P(("rep", "grp", "mem"), None, None),
        ),
        check_vma=False,
    )
```
